256 devices in a mesh: seq: 8 (over x, core), head: 32 (over y, z).
Axes of the slice: x: 4, y: 4, z: 8, core: 2. Of those that a mesh axis runs over, the one named last changes fastest.
Arguments:
- x_inner: bfloat16 [4096, 16384], P('seq', 'head'), may hold values from -6 to 6
- bc_proj: bfloat16 [4096, 4096], P('seq'), may hold values from -6 to 6
- z_gate: bfloat16 [4096, 16384], P('seq', 'head'), may hold values from -6 to 6
- dt_step: float32 [256, 4096], P('head', 'seq'), may hold values from 0.5 to 2
- decay_rate: float32 [256], P('head'), may hold values from 0 to 0.04, as said below
- conv_x_w: bfloat16 [4, 16384], P(None, 'head'), may hold values from -3 to 3
- conv_bc_w: bfloat16 [4, 4096], replicated, may hold values from -3 to 3
- norm_gain: float32 [16384], P('head'), may hold values from 0.5 to 1.5
- out_proj: bfloat16 [16384, 8192], P('head'), may hold values from -0.046875 to 0.046875
Outputs:
- layer_out: bfloat16 [8192, 4096], P('head', 'seq')
The draws below stay inside these ranges and needn't reach their ends.
Inputs may be any that keep to these rules, and one draw needn't show every extreme that they name: `decay_rate`: every rate is positive.
All inputs are finite; a program needn't handle non-finite values.
Results may differ from the reference program's by a relative error of at most 0.025.
Values may be sent and summed in bfloat16 or wider, within the bound.
No kernel may reach another device: no remote copies, remote signals or barrier semaphores. Data moves between devices by JAX's collectives and lax.ppermute only.
A program may use at most 64 MiB of HBM per device.

```python
import math
import jax
import jax.numpy as jnp
from jax import lax

D = 8192
HEADS = 256
HEAD_DIM = 64
STATE = 256
GROUPS = 8
CONV = 4
SPAN = 256
TOKENS = 4096
D_INNER = 16384
N_HEAD = 32


def draw_decay_rate(key, part):
    key_pick, key_slow, key_fast = jax.random.split(jax.random.fold_in(key, 11), 3)
    slow_share = 0.5
    slow_pick = jax.random.uniform(key_pick, (HEADS,), jnp.float32) < slow_share
    slow_rate = jnp.exp(jax.random.uniform(key_slow, (HEADS,), jnp.float32, jnp.log(0.3), jnp.log(0.6))) / (1.08 * TOKENS)
    fast_rate = jnp.exp(jax.random.uniform(key_fast, (HEADS,), jnp.float32, jnp.log(1.0 / 50.0), jnp.log(1.0 / 30.0))) / 1.08
    return jnp.where(slow_pick, slow_rate, fast_rate).astype(jnp.float32)


def steps_of(rng, extent, cuts, least, top_value):
    level, own = 1.0, jax.random.fold_in(rng, 6)
    for dim, parts in cuts:
        draws = jnp.exp(jax.random.uniform(jax.random.fold_in(own, dim), (parts,), jnp.float32, least / len(cuts), top_value / len(cuts)))
        level = level * jnp.repeat(draws, extent[dim] // parts).reshape([-1 if axis == dim else 1 for axis in range(len(extent))])
    return level


def normal_values(rng, extent, scale, reach, cuts=(), held_as=jnp.bfloat16):
    level = steps_of(rng, extent, cuts, -0.22, 0.18) if cuts else 1.0
    entries = jax.random.normal(rng, extent, jnp.float32) * scale * level
    return jnp.minimum(jnp.maximum(entries, -reach), reach).astype(held_as)


def setup_inputs(seed: int = 0) -> dict:
    seeds = jax.random.split(jax.random.key(seed), 10)
    return {
        "x_inner": normal_values(seeds[0], (TOKENS, D_INNER), 1.0, 6.0, ((0, 8), (1, 32))),
        "bc_proj": normal_values(seeds[1], (TOKENS, GROUPS * 2 * STATE), 1.0, 6.0, ((0, 8),)),
        "z_gate": normal_values(seeds[2], (TOKENS, D_INNER), 1.0, 6.0, ((0, 8), (1, 32))),
        "dt_step": jnp.clip(jnp.exp(math.log(2.0) - 1.3862944 * jax.random.uniform(seeds[3], (HEADS, TOKENS), jnp.float32) ** steps_of(seeds[3], (HEADS, TOKENS), ((0, 32), (1, 8)), -0.2, 0.2)), 0.5, 2.0),
        "decay_rate": draw_decay_rate(jax.random.fold_in(seeds[9], 71), 0),
        "conv_x_w": normal_values(seeds[5], (CONV, D_INNER), CONV ** -0.5, 3.0, ((1, 32),)),
        "conv_bc_w": normal_values(seeds[6], (CONV, GROUPS * 2 * STATE), CONV ** -0.5, 3.0),
        "norm_gain": jnp.clip(1.0 + 0.1 * jax.random.normal(seeds[7], (D_INNER,), jnp.float32), 0.5, 1.5),
        "out_proj": normal_values(seeds[8], (D_INNER, D), D_INNER ** -0.5, 0.046875, ((0, 32),)),
    }


norm_eps = 1e-05

def causal(extended, weight, tok_rows):
    running = jnp.zeros((tok_rows, extended.shape[1]), jnp.float32)
    for tap_idx in range(weight.shape[0]):
        running = running + weight[tap_idx].astype(jnp.float32)[None, :] * extended[tap_idx:tap_idx + tok_rows].astype(jnp.float32)
    return jax.nn.silu(running).astype(jnp.bfloat16)

def reference(x_inner, bc_proj, z_gate, dt_step, decay_rate, conv_x_w, conv_bc_w, norm_gain, out_proj):
    rim_rows = CONV - 1
    x_conv = causal(jnp.concatenate([jnp.zeros((rim_rows, x_inner.shape[1]), jnp.bfloat16), x_inner], 0), conv_x_w, TOKENS)
    bc_conv = causal(jnp.concatenate([jnp.zeros((rim_rows, bc_proj.shape[1]), jnp.bfloat16), bc_proj], 0), conv_bc_w, TOKENS)
    n_spans = TOKENS // SPAN
    causal_mask = jnp.arange(SPAN)[:, None] >= jnp.arange(SPAN)[None, :]

    def one_head(head_idx):
        head_idx = head_idx.astype(jnp.int32)
        my_group = head_idx // (HEADS // GROUPS)
        bc_group = lax.dynamic_slice_in_dim(bc_conv, my_group * (2 * STATE), 2 * STATE, 1)
        b_part = bc_group[:, :STATE].reshape(n_spans, SPAN, STATE)
        c_part = bc_group[:, STATE:].reshape(n_spans, SPAN, STATE)
        x_head = lax.dynamic_slice_in_dim(x_conv, head_idx * HEAD_DIM, HEAD_DIM, 1).reshape(n_spans, SPAN, HEAD_DIM)
        dt_head = lax.dynamic_slice_in_dim(dt_step, head_idx, 1, 0).reshape(n_spans, SPAN)
        rate_head = lax.dynamic_slice_in_dim(decay_rate, head_idx, 1, 0)[0]

        def advance(running, span_in):
            x_c, b_c, c_c, dt_c = span_in
            cum_log = jnp.cumsum(-rate_head * dt_c)
            scores = jnp.dot(c_c, b_c.T, preferred_element_type=jnp.float32)
            gap_log = cum_log[:, None] - cum_log[None, :]
            decay_mask = jnp.where(causal_mask, jnp.exp(jnp.where(causal_mask, gap_log, 0.0)), 0.0)
            weights = (scores * decay_mask * dt_c[None, :]).astype(jnp.bfloat16)
            y_diag = jnp.dot(weights, x_c, preferred_element_type=jnp.float32)
            y_off = jnp.exp(cum_log)[:, None] * jnp.dot(c_c.astype(jnp.float32), running.T, precision=lax.Precision.HIGHEST)
            tail_decay = jnp.exp(cum_log[-1] - cum_log) * dt_c
            weighted_b = (tail_decay[:, None] * b_c.astype(jnp.float32)).astype(jnp.bfloat16)
            fresh = jnp.dot(x_c.T, weighted_b, preferred_element_type=jnp.float32)
            return (jnp.exp(cum_log[-1]) * running + fresh, y_diag + y_off)
        end_state, y_head = lax.scan(advance, jnp.zeros((HEAD_DIM, STATE), jnp.float32), (x_head, b_part, c_part, dt_head))
        return y_head.reshape(TOKENS, HEAD_DIM)
    head_out = lax.map(one_head, jnp.arange(HEADS, dtype=jnp.int32))
    y_all = jnp.transpose(head_out, (1, 0, 2)).reshape(TOKENS, HEADS * HEAD_DIM)
    gated = y_all * jax.nn.silu(z_gate.astype(jnp.float32))
    grouped = gated.reshape(TOKENS, GROUPS, -1)
    mean_sq = lax.optimization_barrier(jnp.mean(grouped * grouped, axis=2, keepdims=True))
    normed = ((grouped * lax.rsqrt(mean_sq + norm_eps)).reshape(TOKENS, -1) * norm_gain[None, :]).astype(jnp.bfloat16)
    shard_width = HEADS * HEAD_DIM // N_HEAD

    def add_shard(shard_idx, summed):
        start = jnp.asarray(shard_idx).astype(jnp.int32) * shard_width
        slab_in = lax.dynamic_slice_in_dim(normed, start, shard_width, 1)
        slab_w = lax.dynamic_slice_in_dim(out_proj, start, shard_width, 0)
        rounded = lax.optimization_barrier(jnp.dot(slab_in, slab_w, preferred_element_type=jnp.float32).astype(jnp.bfloat16))
        return summed + rounded.astype(jnp.float32)
    summed = lax.fori_loop(0, N_HEAD, add_shard, jnp.zeros((TOKENS, D), jnp.float32))
    return summed.astype(jnp.bfloat16).T
```

```python
import functools

import jax
import jax.numpy as jnp
from jax import lax
from jax.experimental import pallas as pl
from jax.experimental.pallas import tpu as pltpu
from jax.sharding import PartitionSpec as P

GROUPS = 8
SPAN = 256
CORES = 2
NX = 4
NY = 4
NZ = 8
QUAD = 4
RIM = 16

norm_eps = 1e-05
F32 = jnp.float32
BF16 = jnp.bfloat16
EXACT = lax.Precision.HIGHEST


def y_route(dist):
    return [(y * NZ + z, (y + dist) % NY * NZ + z) for y in range(NY) for z in range(NZ)]


def z_route(dist):
    return [(y * NZ + z, y * NZ + (z + dist) % NZ) for y in range(NY) for z in range(NZ)]


def quad_route(dist):
    return [(h, h // QUAD * QUAD + (h + dist) % QUAD) for h in range(NY * NZ)]


def x_route(dist):
    return [(s, s + CORES * dist) for s in range(NX * CORES) if s + CORES * dist < NX * CORES]


CORE_SWAP = [(s, s ^ 1) for s in range(NX * CORES)]


def dot(a, b, dims=((1,), (0,)), precision=None):
    return lax.dot_general(a, b, (dims, ((), ())), precision=precision, preferred_element_type=F32)


def spread(heads_rows, width):
    heads = heads_rows.shape[0]
    pick = lax.broadcasted_iota(jnp.int32, (heads, width), 1) // (width // heads)
    own = lax.broadcasted_iota(jnp.int32, (heads, width), 0)
    return dot(heads_rows, (pick == own).astype(F32), ((0,), (0,)), EXACT)


def conv(buf, src_ref, rim, w_ref):
    rows = src_ref.shape[0]
    buf[0:8] = rim
    buf[8 : rows + 8] = src_ref[...].astype(F32)
    taps = w_ref[...].astype(F32)
    run = taps[0:1] * buf[5 : 5 + rows]
    for k in range(1, 4):
        run = run + taps[k : k + 1] * buf[5 + k : 5 + k + rows]
    return (run * jax.nn.sigmoid(run)).astype(BF16)


def state_kernel(
    at_ref, x_ref, bc_ref, rim_ref, wx_ref, wbc_ref, dt_ref, rate_ref,
    pay_ref, xs_ref, bc_out, s0_ref, ec_ref, e0_ref, xbuf, bbuf,
):
    width = x_ref.shape[1]
    rows = x_ref.shape[0]
    state = bc_ref.shape[1] // 2
    rim = rim_ref[...].astype(F32)[RIM - 8 :]
    x_conv = conv(xbuf, x_ref, rim[:, :width], wx_ref)
    bc = conv(bbuf, bc_ref, rim[:, width:], wbc_ref)
    bc_out[...] = bc
    dt = dt_ref[...]
    steps = -rate_ref[...] * dt
    before = (
        lax.broadcasted_iota(jnp.int32, (SPAN, SPAN), 0)
        <= lax.broadcasted_iota(jnp.int32, (SPAN, SPAN), 1)
    ).astype(F32)
    cum = jnp.concatenate(
        [dot(steps[:, s : s + SPAN], before, precision=EXACT) for s in range(0, rows, SPAN)], 1
    )
    grow = jnp.exp(cum)
    ec_ref[...] = grow
    scale = spread(dt * jnp.exp(-cum), width)
    xs = (x_conv.astype(F32) * scale).astype(BF16)
    xs_ref[...] = xs
    b_all = bc[:, :state]
    lasts = jnp.concatenate([grow[:, SPAN - 1 : SPAN], grow[:, rows - 1 : rows]], 1)
    last = spread(lasts, width)
    s0 = last[0:1] * dot(b_all[:SPAN], xs[:SPAN], ((0,), (0,)))
    s1 = last[1:2] * dot(b_all[SPAN:], xs[SPAN:], ((0,), (0,)))
    s0_ref[...] = s0.astype(BF16)
    e0_ref[...] = jnp.broadcast_to(last[0:1], e0_ref.shape)
    pay_ref[0:state] = (last[1:2] * s0 + s1).astype(BF16)
    whole = last[0:1] * last[1:2]
    pay_ref[state : state + 16] = decay_rows(whole)


def decay_rows(whole):
    top = whole.astype(BF16).astype(F32)
    mid = (whole - top).astype(BF16).astype(F32)
    low = whole - top - mid
    row = lax.broadcasted_iota(jnp.int32, (16, whole.shape[1]), 0)
    zero = jnp.zeros_like(row, F32)
    return jnp.where(
        row == 0, top, jnp.where(row == 1, mid, jnp.where(row == 2, low, zero))
    ).astype(BF16)


def decay_of(payload, state):
    rows = payload[state : state + 16].astype(F32)
    return rows[0:1] + rows[1:2] + rows[2:3]


def chip_kernel(at_ref, own_ref, other_ref, out_ref):
    core = at_ref[1]
    half = out_ref.shape[1]
    state = own_ref.shape[0] - 16
    cols = pl.ds(pl.multiple_of(core * half, half), half)
    own, other = own_ref[:, cols], other_ref[:, cols]
    own_decay, other_decay = decay_of(own, state), decay_of(other, state)
    own_s, other_s = own[:state].astype(F32), other[:state].astype(F32)
    late = jnp.where(core == 1, own_decay, other_decay)
    first = jnp.where(core == 1, other_s, own_s)
    second = jnp.where(core == 1, own_s, other_s)
    out_ref[0:state] = (late * first + second).astype(BF16)
    out_ref[state : state + 16] = decay_rows(own_decay * other_decay)


def prefix_kernel(one_ref, two_ref, three_ref, out_ref):
    state = out_ref.shape[0]
    one, two, three = one_ref[...], two_ref[...], three_ref[...]
    total = two[:state].astype(F32) + decay_of(two, state) * three[:state].astype(F32)
    total = one[:state].astype(F32) + decay_of(one, state) * total
    out_ref[...] = total.astype(BF16)


def diag_kernel(xs_ref, bc_ref, s0_ref, ec_ref, z_ref, y_ref, gate_ref):
    rows, width = xs_ref.shape
    state = bc_ref.shape[1] // 2
    seen = lax.broadcasted_iota(jnp.int32, (SPAN, SPAN), 0) >= lax.broadcasted_iota(
        jnp.int32, (SPAN, SPAN), 1
    )
    for s in range(0, rows, SPAN):
        b, c = bc_ref[s : s + SPAN, :state], bc_ref[s : s + SPAN, state:]
        scores = jnp.where(seen, dot(c, b, ((1,), (1,))), 0.0).astype(BF16)
        y = dot(scores, xs_ref[s : s + SPAN])
        if s:
            y = y + dot(c, s0_ref[...])
        y_ref[s : s + SPAN] = y
    z = z_ref[...].astype(F32)
    gate_ref[...] = z * jax.nn.sigmoid(z) * spread(ec_ref[...], width)


def gate_kernel(
    at_ref, mine_ref, theirs_ref, other_ref, bc_ref, y_ref, gate_ref, e0_ref, out_ref, ss_ref
):
    core = at_ref[1]
    state, half = mine_ref.shape
    rows = bc_ref.shape[0]
    mine, theirs = mine_ref[...].astype(F32), theirs_ref[...].astype(F32)
    left = jnp.where(core == 0, mine, theirs)
    right = jnp.where(core == 0, theirs, mine)
    prior = jnp.concatenate([left, right], 1)
    other = other_ref[...]
    after = decay_of(other, state) * prior + other[:state].astype(F32)
    incoming = jnp.where(core == 1, after, prior)
    ss = jnp.zeros(ss_ref.shape[:1] + (SPAN,), F32)
    ones = jnp.ones((8, out_ref.shape[1]), F32)
    for n, s in enumerate(range(0, rows, SPAN)):
        start = incoming if n == 0 else incoming * e0_ref[0:1]
        y = y_ref[s : s + SPAN] + dot(bc_ref[s : s + SPAN, state:], start.astype(BF16))
        gated = y * gate_ref[s : s + SPAN]
        out_ref[s : s + SPAN] = gated
        ss_ref[:, s : s + SPAN] = dot(ones, gated * gated, ((1,), (1,)), EXACT)


def norm_kernel(group_width, gated_ref, gain_ref, s0_ref, s1_ref, s2_ref, s3_ref, out_ref):
    mean_sq = (s0_ref[...] + s1_ref[...] + s2_ref[...] + s3_ref[...]) / group_width
    scale = spread(lax.rsqrt(mean_sq + norm_eps)[0:1], out_ref.shape[1])
    out_ref[...] = (gated_ref[...] * scale * gain_ref[...]).astype(BF16)


def project_kernel(
    at_ref, n0_ref, n1_ref, n2_ref, n3_ref, w0_ref, w1_ref, w2_ref, w3_ref, v1_ref, v2_ref, v3_ref, out_ref
):
    core = at_ref[1]
    half = w1_ref.shape[0]
    mine = pl.ds(pl.multiple_of(core * half, half), half)
    theirs = pl.ds(pl.multiple_of((1 - core) * half, half), half)
    total = dot(n0_ref[...], w0_ref[...])
    for n, w, v in ((n1_ref, w1_ref, v1_ref), (n2_ref, w2_ref, v2_ref), (n3_ref, w3_ref, v3_ref)):
        total = total + dot(n[:, mine], w[...])
        total = total + dot(n[:, theirs], v[...])
    out_ref[0] = total.astype(BF16)


def call(body, at, ins, outs, scratch=(), specs=None, grid=(1,), out_specs=None, flops=0):
    full = lambda s: pl.BlockSpec(s, lambda *_, n=len(s): (0,) * n)
    specs = specs or {}
    in_specs = [specs.get(k) or full(a.shape) for k, a in enumerate(ins)]
    kwargs = dict(
        out_shape=outs,
        compiler_params=pltpu.CompilerParams(vmem_limit_bytes=48 << 20),
        cost_estimate=pl.CostEstimate(
            flops=flops,
            bytes_accessed=sum(a.size * a.dtype.itemsize for a in (*ins, *outs)),
            transcendentals=0,
        ),
    )
    if out_specs is None:
        out_specs = [full(o.shape) for o in outs]
    if at is None:
        return pl.pallas_call(
            body, grid=grid, in_specs=in_specs, out_specs=out_specs, scratch_shapes=scratch, **kwargs
        )(*ins)
    return pl.pallas_call(
        body,
        grid_spec=pltpu.PrefetchScalarGridSpec(
            num_scalar_prefetch=1, grid=grid, in_specs=in_specs, out_specs=out_specs, scratch_shapes=scratch
        ),
        **kwargs,
    )(at, *ins)


def like(shape, dtype):
    return jax.ShapeDtypeStruct(shape, dtype)


def on_device(x, bc, z_gate, dt, rate, wx, wbc, gain, w_out):
    rows, width = x.shape
    heads = rate.shape[0]
    cols = bc.shape[1] // GROUPS
    state = cols // 2
    head_at, seq_at = lax.axis_index("head"), lax.axis_index("seq")
    group, core, y_at, z_at = head_at // QUAD, seq_at % CORES, head_at // NZ, head_at % NZ
    at = jnp.stack([group, core, y_at, z_at]).astype(jnp.int32)

    edge = lax.dynamic_slice(bc, (rows - RIM, group * cols), (RIM, cols))
    rim = lax.ppermute(
        jnp.concatenate([x[rows - RIM :], edge], 1), "seq", [(s, s + 1) for s in range(7)]
    )

    quarter = w_out.shape[1] // NY
    half_k = width // CORES
    w_mine = [
        lax.ppermute(
            lax.dynamic_slice(w_out, (core * half_k, (y_at + d) % NY * quarter), (half_k, quarter)),
            "head",
            y_route(d),
        )
        for d in range(1, NY)
    ]
    w_theirs = [lax.ppermute(w, "seq", CORE_SWAP) for w in w_mine]

    block = pl.BlockSpec((rows, cols), lambda i, s: (0, s[0]))
    wblock = pl.BlockSpec((4, cols), lambda i, s: (0, s[0]))
    payload, xs, bc_conv, s0, grow, e0 = call(
        state_kernel,
        at,
        [x, bc, rim, wx, wbc, dt, rate[:, None]],
        [
            like((state + 16, width), BF16),
            like((rows, width), BF16),
            like((rows, cols), BF16),
            like((state, width), BF16),
            like((heads, rows), F32),
            like((8, width), F32),
        ],
        scratch=[pltpu.VMEM((rows + 8, width), F32), pltpu.VMEM((rows + 8, cols), F32)],
        specs={1: block, 4: wblock},
    )
    other = lax.ppermute(payload, "seq", CORE_SWAP)
    [chip] = call(chip_kernel, at, [payload, other], [like((state + 16, width // 2), BF16)])
    befores = [lax.ppermute(chip, "seq", x_route(d)) for d in (1, 2, 3)]
    y_local, gate = call(
        diag_kernel,
        None,
        [xs, bc_conv, s0, grow, z_gate],
        [like((rows, width), F32), like((rows, width), F32)],
    )
    [mine] = call(prefix_kernel, None, befores, [like((state, width // 2), BF16)])
    theirs = lax.ppermute(mine, "seq", CORE_SWAP)
    gated, ss = call(
        gate_kernel,
        at,
        [mine, theirs, other, bc_conv, y_local, gate, e0],
        [like((rows, width), F32), like((8, rows), F32)],
    )
    more = [lax.ppermute(ss, "head", quad_route(d)) for d in range(1, QUAD)]
    [normed] = call(
        functools.partial(norm_kernel, width * QUAD),
        None,
        [gated, gain[None, :], ss, *more],
        [like((rows, width), BF16)],
    )
    peers = [lax.ppermute(normed, "head", y_route(d)) for d in range(1, NY)]
    feats = quarter // NZ
    in_quarter = pl.BlockSpec((half_k, feats), lambda i, s: (0, (s[3] + i) % NZ))
    in_whole = pl.BlockSpec((width, feats), lambda i, s: (0, s[2] * NZ + (s[3] + i) % NZ))
    [parts] = call(
        project_kernel,
        at,
        [normed, *peers, w_out, *w_mine, *w_theirs],
        [like((NZ, rows, feats), BF16)],
        specs={4: in_whole, **{k: in_quarter for k in range(5, 11)}},
        grid=(NZ,),
        out_specs=[pl.BlockSpec((1, rows, feats), lambda i, s: (i, 0, 0))],
        flops=2 * rows * width * quarter * NY,
    )
    send = lambda v, d: lax.ppermute(v, "head", z_route(d))
    mid = rows // 2
    up, down = send(parts[4, :mid], 1), send(parts[4, mid:], -1)
    add = lambda a, b: (a.astype(F32) + b.astype(F32)).astype(BF16)
    up = send(jnp.concatenate([add(parts[3, :mid], up), parts[3, mid:]], 0), 1)
    down = send(jnp.concatenate([parts[5, :mid], add(parts[5, mid:], down)], 0), -1)
    up, down = send(add(parts[2], up), 1), send(add(parts[6], down), -1)
    up, down = send(add(parts[1], up), 1), send(add(parts[7], down), -1)
    return (parts[0].astype(F32) + up.astype(F32) + down.astype(F32)).astype(BF16).T


def solution(mesh):
    placed = (
        P("seq", "head"),
        P("seq", None),
        P("seq", "head"),
        P("head", "seq"),
        P("head"),
        P(None, "head"),
        P(),
        P("head"),
        P("head", None),
    )
    return jax.shard_map(
        on_device, mesh=mesh, in_specs=placed, out_specs=P("head", "seq"), check_vma=False
    )
```

```python
import functools

import jax
import jax.numpy as jnp
from jax import lax
from jax.experimental import pallas as pl
from jax.experimental.pallas import tpu as pltpu
from jax.sharding import PartitionSpec as P

GROUPS = 8
SPAN = 256
CORES = 2
NX = 4
NY = 4
NZ = 8
QUAD = 4
RIM = 16

norm_eps = 1e-05
F32 = jnp.float32
BF16 = jnp.bfloat16
EXACT = lax.Precision.HIGHEST


def y_route(dist):
    return [(y * NZ + z, (y + dist) % NY * NZ + z) for y in range(NY) for z in range(NZ)]


def z_route(dist):
    return [(y * NZ + z, y * NZ + (z + dist) % NZ) for y in range(NY) for z in range(NZ)]


def quad_route(dist):
    return [(h, h // QUAD * QUAD + (h + dist) % QUAD) for h in range(NY * NZ)]


def x_route(dist):
    return [(s, s + CORES * dist) for s in range(NX * CORES) if s + CORES * dist < NX * CORES]


CORE_SWAP = [(s, s ^ 1) for s in range(NX * CORES)]


def dot(a, b, dims=((1,), (0,)), precision=None):
    return lax.dot_general(a, b, (dims, ((), ())), precision=precision, preferred_element_type=F32)


def spread(heads_rows, width):
    heads = heads_rows.shape[0]
    pick = lax.broadcasted_iota(jnp.int32, (heads, width), 1) // (width // heads)
    own = lax.broadcasted_iota(jnp.int32, (heads, width), 0)
    return dot(heads_rows, (pick == own).astype(F32), ((0,), (0,)), EXACT)


def conv(buf, src_ref, rim, w_ref):
    rows = src_ref.shape[0]
    buf[0:8] = rim
    buf[8 : rows + 8] = src_ref[...].astype(F32)
    taps = w_ref[...].astype(F32)
    run = taps[0:1] * buf[5 : 5 + rows]
    for k in range(1, 4):
        run = run + taps[k : k + 1] * buf[5 + k : 5 + k + rows]
    return (run * jax.nn.sigmoid(run)).astype(BF16)


def state_kernel(
    at_ref, x_ref, bc_ref, rim_ref, wx_ref, wbc_ref, dt_ref, rate_ref,
    pay_ref, xs_ref, bc_out, s0_ref, ec_ref, e0_ref, xbuf, bbuf,
):
    width = x_ref.shape[1]
    rows = x_ref.shape[0]
    state = bc_ref.shape[1] // 2
    rim = rim_ref[...].astype(F32)[RIM - 8 :]
    x_conv = conv(xbuf, x_ref, rim[:, :width], wx_ref)
    bc = conv(bbuf, bc_ref, rim[:, width:], wbc_ref)
    bc_out[...] = bc
    dt = dt_ref[...]
    own_row = lax.broadcasted_iota(jnp.int32, (dt.shape[0],) * 2, 0)
    own_row = own_row == lax.broadcasted_iota(jnp.int32, own_row.shape, 1)
    rate = jnp.sum(jnp.where(own_row, rate_ref[...], 0.0), 1, keepdims=True)
    steps = -rate * dt
    before = (
        lax.broadcasted_iota(jnp.int32, (SPAN, SPAN), 0)
        <= lax.broadcasted_iota(jnp.int32, (SPAN, SPAN), 1)
    ).astype(F32)
    cum = jnp.concatenate(
        [dot(steps[:, s : s + SPAN], before, precision=EXACT) for s in range(0, rows, SPAN)], 1
    )
    grow = jnp.exp(cum)
    ec_ref[...] = grow
    scale = spread(dt * jnp.exp(-cum), width)
    xs = (x_conv.astype(F32) * scale).astype(BF16)
    xs_ref[...] = xs
    b_all = bc[:, :state]
    lasts = jnp.concatenate([grow[:, SPAN - 1 : SPAN], grow[:, rows - 1 : rows]], 1)
    last = spread(lasts, width)
    s0 = last[0:1] * dot(b_all[:SPAN], xs[:SPAN], ((0,), (0,)))
    s1 = last[1:2] * dot(b_all[SPAN:], xs[SPAN:], ((0,), (0,)))
    s0_ref[...] = s0.astype(BF16)
    e0_ref[...] = jnp.broadcast_to(last[0:1], e0_ref.shape)
    pay_ref[0:state] = (last[1:2] * s0 + s1).astype(BF16)
    whole = last[0:1] * last[1:2]
    pay_ref[state : state + 16] = decay_rows(whole)


def decay_rows(whole):
    top = whole.astype(BF16).astype(F32)
    mid = (whole - top).astype(BF16).astype(F32)
    low = whole - top - mid
    row = lax.broadcasted_iota(jnp.int32, (16, whole.shape[1]), 0)
    zero = jnp.zeros_like(row, F32)
    return jnp.where(
        row == 0, top, jnp.where(row == 1, mid, jnp.where(row == 2, low, zero))
    ).astype(BF16)


def decay_of(payload, state):
    rows = payload[state : state + 16].astype(F32)
    return rows[0:1] + rows[1:2] + rows[2:3]


def chip_kernel(at_ref, own_ref, other_ref, out_ref):
    core = at_ref[1]
    half = out_ref.shape[1]
    state = own_ref.shape[0] - 16
    cols = pl.ds(pl.multiple_of(core * half, half), half)
    own, other = own_ref[:, cols], other_ref[:, cols]
    own_decay, other_decay = decay_of(own, state), decay_of(other, state)
    own_s, other_s = own[:state].astype(F32), other[:state].astype(F32)
    late = jnp.where(core == 1, own_decay, other_decay)
    first = jnp.where(core == 1, other_s, own_s)
    second = jnp.where(core == 1, own_s, other_s)
    out_ref[0:state] = (late * first + second).astype(BF16)
    out_ref[state : state + 16] = decay_rows(own_decay * other_decay)


def prefix_kernel(one_ref, two_ref, three_ref, out_ref):
    state = out_ref.shape[0]
    one, two, three = one_ref[...], two_ref[...], three_ref[...]
    total = two[:state].astype(F32) + decay_of(two, state) * three[:state].astype(F32)
    total = one[:state].astype(F32) + decay_of(one, state) * total
    out_ref[...] = total.astype(BF16)


def diag_kernel(xs_ref, bc_ref, s0_ref, ec_ref, z_ref, y_ref, gate_ref):
    rows, width = xs_ref.shape
    state = bc_ref.shape[1] // 2
    seen = lax.broadcasted_iota(jnp.int32, (SPAN, SPAN), 0) >= lax.broadcasted_iota(
        jnp.int32, (SPAN, SPAN), 1
    )
    for s in range(0, rows, SPAN):
        b, c = bc_ref[s : s + SPAN, :state], bc_ref[s : s + SPAN, state:]
        scores = jnp.where(seen, dot(c, b, ((1,), (1,))), 0.0).astype(BF16)
        y = dot(scores, xs_ref[s : s + SPAN])
        if s:
            y = y + dot(c, s0_ref[...])
        y_ref[s : s + SPAN] = y
    z = z_ref[...].astype(F32)
    gate_ref[...] = z * jax.nn.sigmoid(z) * spread(ec_ref[...], width)


def gate_kernel(
    at_ref, mine_ref, theirs_ref, other_ref, bc_ref, y_ref, gate_ref, e0_ref, out_ref, ss_ref
):
    core = at_ref[1]
    state, half = mine_ref.shape
    mine, theirs = mine_ref[...].astype(F32), theirs_ref[...].astype(F32)
    left = jnp.where(core == 0, mine, theirs)
    right = jnp.where(core == 0, theirs, mine)
    prior = jnp.concatenate([left, right], 1)
    other = other_ref[...]
    after = decay_of(other, state) * prior + other[:state].astype(F32)
    incoming = jnp.where(core == 1, after, prior)
    ones = jnp.ones((8, out_ref.shape[1]), F32)
    for n, s in enumerate(range(0, bc_ref.shape[0], SPAN)):
        start = incoming if n == 0 else incoming * e0_ref[0:1]
        y = y_ref[s : s + SPAN] + dot(bc_ref[s : s + SPAN, state:], start.astype(BF16))
        gated = y * gate_ref[s : s + SPAN]
        out_ref[s : s + SPAN] = gated
        ss_ref[:, s : s + SPAN] = dot(ones, gated * gated, ((1,), (1,)), EXACT)


def part_order(px, core):
    return [2 * px + core, 2 * px + 1 - core, 2 * (1 - px) + core, 2 * (1 - px) + 1 - core]


def ahead_kernel(at_ref, *refs):
    out_ref = refs[-1]
    feats = out_ref.shape[3]
    for y, w_ref in enumerate(refs[:-1]):
        for j in range(out_ref.shape[1]):
            out_ref[y, j] = w_ref[:, j * feats : (j + 1) * feats]


def sort_kernel(at_ref, one_ref, two_ref, three_ref, all_ref, low_ref, high_ref):
    half = low_ref.shape[2]
    for d, ref in enumerate((one_ref, two_ref, three_ref)):
        piece = ref[0]
        all_ref[d] = piece
        low_ref[d] = piece[:, :half]
        high_ref[d] = piece[:, half:]


def norm_kernel(group_width, gated_ref, gain_ref, s0_ref, s1_ref, s2_ref, s3_ref, out_ref):
    mean_sq = (s0_ref[...] + s1_ref[...] + s2_ref[...] + s3_ref[...]) / group_width
    scale = spread(lax.rsqrt(mean_sq + norm_eps)[0:1], 128)
    for k in range(0, out_ref.shape[1], 128):
        piece = gated_ref[:, k : k + 128] * scale * gain_ref[:, k : k + 128]
        out_ref[:, k : k + 128] = piece.astype(BF16)


def project_kernel(at_ref, n0_ref, n1_ref, low_ref, high_ref, n3_ref, w0_ref, *refs):
    pieces, out_refs = refs[:6], refs[6:]
    part = n0_ref.shape[1] // 4
    rows, weights = [n0_ref[...]], [w0_ref[...]]
    for d, n_refs in enumerate(((n1_ref,), (low_ref, high_ref), (n3_ref,))):
        for p in part_order(at_ref[4], at_ref[1]):
            cols = pl.ds(pl.multiple_of(p * part, part), part)
            rows.append(jnp.concatenate([n[:, cols] for n in n_refs], 0))
        weights += [p[d, 0] for p in pieces]
    total = dot(jnp.concatenate(rows, 1), jnp.concatenate(weights, 0))
    if len(out_refs) == 1:
        out_refs[0][0] = total.astype(BF16)
    else:
        mid = out_refs[0].shape[0]
        out_refs[0][...] = total[:mid].astype(BF16)
        out_refs[1][...] = total[mid:].astype(BF16)


def call(body, at, ins, outs, scratch=(), specs=None, grid=(1,), out_specs=None, flops=0, vmem=48):
    full = lambda s: pl.BlockSpec(s, lambda *_, n=len(s): (0,) * n)
    specs = specs or {}
    in_specs = [specs.get(k) or full(a.shape) for k, a in enumerate(ins)]
    kwargs = dict(
        out_shape=outs,
        compiler_params=pltpu.CompilerParams(vmem_limit_bytes=vmem << 20),
        cost_estimate=pl.CostEstimate(
            flops=flops,
            bytes_accessed=sum(a.size * a.dtype.itemsize for a in (*ins, *outs)),
            transcendentals=0,
        ),
    )
    if out_specs is None:
        out_specs = [full(o.shape) for o in outs]
    if at is None:
        return pl.pallas_call(
            body, grid=grid, in_specs=in_specs, out_specs=out_specs, scratch_shapes=scratch, **kwargs
        )(*ins)
    return pl.pallas_call(
        body,
        grid_spec=pltpu.PrefetchScalarGridSpec(
            num_scalar_prefetch=1, grid=grid, in_specs=in_specs, out_specs=out_specs, scratch_shapes=scratch
        ),
        **kwargs,
    )(at, *ins)


def like(shape, dtype):
    return jax.ShapeDtypeStruct(shape, dtype)


def on_device(x, bc, z_gate, dt, rate, wx, wbc, gain, w_out):
    rows, width = x.shape
    heads = rate.shape[0]
    cols = bc.shape[1] // GROUPS
    state = cols // 2
    head_at, seq_at = lax.axis_index("head"), lax.axis_index("seq")
    group, core, y_at, z_at = head_at // QUAD, seq_at % CORES, head_at // NZ, head_at % NZ
    at = jnp.stack([group, core, y_at, z_at, seq_at // CORES % 2]).astype(jnp.int32)

    edge = lax.dynamic_slice(bc, (rows - RIM, group * cols), (RIM, cols))
    edges = jnp.concatenate([x[rows - RIM :], edge], 1)
    rim = lax.ppermute(edges, "seq", [(s, s + 1) for s in range(7)])

    quarter = w_out.shape[1] // NY
    feats = quarter // NZ
    part_k = width // 4
    at_late, _ = lax.optimization_barrier((at, edges))
    [ahead] = call(
        ahead_kernel,
        at_late,
        [w_out] * NY,
        [like((NY, NZ, part_k, feats), BF16)],
        specs={
            y: pl.BlockSpec((part_k, quarter), lambda i, s, y=y: (2 * s[4] + s[1], y))
            for y in range(NY)
        },
    )
    rim, ahead = lax.optimization_barrier((rim, ahead))
    columns = [[y * NZ + z for y in range(NY)] for z in range(NZ)]
    arrived = lax.all_to_all(ahead, "head", 0, 0, tiled=True, axis_index_groups=columns)

    block = pl.BlockSpec((rows, cols), lambda i, s: (0, s[0]))
    wblock = pl.BlockSpec((4, cols), lambda i, s: (0, s[0]))
    payload, xs, bc_conv, s0, grow, e0 = call(
        state_kernel,
        at,
        [x, bc, rim, wx, wbc, dt, rate[None, :]],
        [
            like((state + 16, width), BF16),
            like((rows, width), BF16),
            like((rows, cols), BF16),
            like((state, width), BF16),
            like((heads, rows), F32),
            like((8, width), F32),
        ],
        scratch=[pltpu.VMEM((rows + 8, width), F32), pltpu.VMEM((rows + 8, cols), F32)],
        specs={1: block, 4: wblock}
    )
    other = lax.ppermute(payload, "seq", CORE_SWAP)
    [chip] = call(chip_kernel, at, [payload, other], [like((state + 16, width // 2), BF16)])
    befores = [lax.ppermute(chip, "seq", x_route(d)) for d in (1, 2, 3)]
    y_local, gate = call(
        diag_kernel,
        None,
        [xs, bc_conv, s0, grow, z_gate],
        [like((rows, width), F32), like((rows, width), F32)],
    )
    [mine] = call(prefix_kernel, None, befores, [like((state, width // 2), BF16)])
    theirs = lax.ppermute(mine, "seq", CORE_SWAP)

    gated, ss = call(
        gate_kernel,
        at,
        [mine, theirs, other, bc_conv, y_local, gate, e0],
        [like((rows, width), F32), like((8, rows), F32)],
    )
    more = [lax.ppermute(ss, "head", quad_route(d)) for d in range(1, QUAD)]
    [normed] = call(
        functools.partial(norm_kernel, width * QUAD),
        None,
        [gated, gain[None, :], ss, *more],
        [like((rows, width), BF16)],
    )
    mid = rows // 2
    near_up, near_down = (lax.ppermute(normed, "head", y_route(d)) for d in (1, -1))
    far_low = lax.ppermute(near_up[:mid], "head", y_route(1))
    far_high = lax.ppermute(near_down[mid:], "head", y_route(-1))
    peers = [near_up, far_low, far_high, near_down]

    at_then, _ = lax.optimization_barrier((at, ss))
    arrived_from = lambda d: pl.BlockSpec(
        (1, NZ, part_k, feats), lambda i, s: ((s[2] + NY - d) % NY, 0, 0, 0)
    )
    pair = (NY - 1, NZ, part_k // 2, feats)
    own, low, high = call(
        sort_kernel,
        at_then,
        [arrived] * (NY - 1),
        [like((NY - 1, NZ, part_k, feats), BF16), like(pair, BF16), like(pair, BF16)],
        specs={d - 1: arrived_from(d) for d in range(1, NY)},
    )
    ring = NX * CORES
    x_low = lax.ppermute(low, "seq", [(s, (s + CORES) % ring) for s in range(ring)])
    x_high = lax.ppermute(high, "seq", [(s, (s - CORES) % ring) for s in range(ring)])
    own_late, _ = lax.optimization_barrier((own, normed))
    swap = lambda v: lax.ppermute(v, "seq", CORE_SWAP)
    pieces = [own, swap(own_late), x_low, x_high, swap(x_low), swap(x_high)]

    def project(order, after):
        at_then, _ = lax.optimization_barrier((at, after))
        turn = lambda i: order[0] + sum(
            (b - a) * (i >= k + 1).astype(jnp.int32) for k, (a, b) in enumerate(zip(order, order[1:]))
        )
        piece = lambda v: pl.BlockSpec(
            (NY - 1, 1, v.shape[2], feats), lambda i, s: (0, (s[3] + turn(i)) % NZ, 0, 0)
        )
        own = pl.BlockSpec((width, feats), lambda i, s: (0, s[2] * NZ + (s[3] + turn(i)) % NZ))
        if len(order) == 1:
            outs, out_specs = [like((rows // 2, feats), BF16)] * 2, None
        else:
            outs = [like((len(order), rows, feats), BF16)]
            out_specs = [pl.BlockSpec((1, rows, feats), lambda i, s: (i, 0, 0))]
        return call(
            project_kernel,
            at_then,
            [normed, *peers, w_out, *pieces],
            outs,
            specs={5: own, **{6 + k: piece(v) for k, v in enumerate(pieces)}},
            grid=(len(order),),
            out_specs=out_specs,
            flops=2 * rows * width * NY * feats * len(order),
        )

    send = lambda v, d: lax.ppermute(v, "head", z_route(d))
    add = lambda a, b: (a.astype(F32) + b.astype(F32)).astype(BF16)
    far_up, far_down = project((4,), normed)
    up, down = send(far_up, 1), send(far_down, -1)
    [third] = project((3, 5), far_up)
    [second] = project((2, 6), (up, down))
    up = send(jnp.concatenate([add(third[0, :mid], up), third[0, mid:]], 0), 1)
    down = send(jnp.concatenate([third[1, :mid], add(third[1, mid:], down)], 0), -1)
    [first] = project((1, 7), (up, down))
    up, down = send(add(second[0], up), 1), send(add(second[1], down), -1)
    own_halves = project((0,), (up, down))
    up, down = send(add(first[0], up), 1), send(add(first[1], down), -1)
    own = jnp.concatenate(own_halves, 0)
    return (own.astype(F32) + up.astype(F32) + down.astype(F32)).astype(BF16).T


def solution(mesh):
    placed = (
        P("seq", "head"),
        P("seq", None),
        P("seq", "head"),
        P("head", "seq"),
        P("head"),
        P(None, "head"),
        P(),
        P("head"),
        P("head", None),
    )
    return jax.shard_map(
        on_device, mesh=mesh, in_specs=placed, out_specs=P("head", "seq"), check_vma=False
    )
```

```python
import functools

import jax
import jax.numpy as jnp
from jax import lax
from jax.experimental import pallas as pl
from jax.experimental.pallas import tpu as pltpu
from jax.sharding import PartitionSpec as P

GROUPS = 8
SPAN = 256
CORES = 2
NX = 4
NY = 4
NZ = 8
QUAD = 4
RIM = 16

norm_eps = 1e-05
F32 = jnp.float32
BF16 = jnp.bfloat16
EXACT = lax.Precision.HIGHEST


def y_route(dist):
    return [(y * NZ + z, (y + dist) % NY * NZ + z) for y in range(NY) for z in range(NZ)]


def z_route(dist):
    return [(y * NZ + z, y * NZ + (z + dist) % NZ) for y in range(NY) for z in range(NZ)]


def quad_route(dist):
    return [(h, h // QUAD * QUAD + (h + dist) % QUAD) for h in range(NY * NZ)]


def x_route(dist):
    return [(s, s + CORES * dist) for s in range(NX * CORES) if s + CORES * dist < NX * CORES]


CORE_SWAP = [(s, s ^ 1) for s in range(NX * CORES)]


def dot(a, b, dims=((1,), (0,)), precision=None):
    return lax.dot_general(a, b, (dims, ((), ())), precision=precision, preferred_element_type=F32)


def thirds(v):
    top = v.astype(BF16)
    rest = v - top.astype(F32)
    mid = rest.astype(BF16)
    return top, mid, (rest - mid.astype(F32)).astype(BF16)


def spread(heads_rows, width):
    heads = heads_rows.shape[0]
    pick = lax.broadcasted_iota(jnp.int32, (heads, width), 1) // (width // heads)
    own = lax.broadcasted_iota(jnp.int32, (heads, width), 0)
    pick = (pick == own).astype(F32)
    pick = jnp.concatenate([pick] * 3, 0).astype(BF16)
    parts = jnp.concatenate([p.astype(F32) for p in thirds(heads_rows)], 0).astype(BF16)
    return dot(parts, pick, ((0,), (0,)))


def conv(buf, src_ref, rim, w_ref):
    rows = src_ref.shape[0]
    buf[0:8] = rim
    buf[8 : rows + 8] = src_ref[...].astype(F32)
    taps = w_ref[...].astype(F32)
    run = taps[0:1] * buf[5 : 5 + rows]
    for k in range(1, 4):
        run = run + taps[k : k + 1] * buf[5 + k : 5 + k + rows]
    return (run * jax.nn.sigmoid(run)).astype(BF16)


def state_kernel(
    at_ref, x_ref, bc_ref, rim_ref, wx_ref, wbc_ref, dt_ref, rate_ref,
    pay_ref, xs_ref, bc_out, s0_ref, ec_ref, e0_ref, xbuf, bbuf,
):
    width = x_ref.shape[1]
    rows = x_ref.shape[0]
    state = bc_ref.shape[1] // 2
    rim = rim_ref[...].astype(F32)[RIM - 8 :]
    x_conv = conv(xbuf, x_ref, rim[:, :width], wx_ref)
    bc = conv(bbuf, bc_ref, rim[:, width:], wbc_ref)
    bc_out[...] = bc
    dt = dt_ref[...]
    own_row = lax.broadcasted_iota(jnp.int32, (dt.shape[0],) * 2, 0)
    own_row = own_row == lax.broadcasted_iota(jnp.int32, own_row.shape, 1)
    rate = jnp.sum(jnp.where(own_row, rate_ref[...], 0.0), 1, keepdims=True)
    steps = -rate * dt
    before = (
        lax.broadcasted_iota(jnp.int32, (SPAN, SPAN), 0)
        <= lax.broadcasted_iota(jnp.int32, (SPAN, SPAN), 1)
    ).astype(F32)
    cum = jnp.concatenate(
        [dot(steps[:, s : s + SPAN], before, precision=EXACT) for s in range(0, rows, SPAN)], 1
    )
    grow = jnp.exp(cum)
    ec_ref[...] = grow
    scale = spread(dt * jnp.exp(-cum), width)
    xs = (x_conv.astype(F32) * scale).astype(BF16)
    xs_ref[...] = xs
    b_all = bc[:, :state]
    lasts = jnp.concatenate([grow[:, SPAN - 1 : SPAN], grow[:, rows - 1 : rows]], 1)
    last = spread(lasts, width)
    s0 = last[0:1] * dot(b_all[:SPAN], xs[:SPAN], ((0,), (0,)))
    s1 = last[1:2] * dot(b_all[SPAN:], xs[SPAN:], ((0,), (0,)))
    s0_ref[...] = s0.astype(BF16)
    e0_ref[...] = jnp.broadcast_to(last[0:1], e0_ref.shape)
    pay_ref[0:state] = (last[1:2] * s0 + s1).astype(BF16)
    whole = last[0:1] * last[1:2]
    pay_ref[state : state + 16] = decay_rows(whole)


def decay_rows(whole):
    top = whole.astype(BF16).astype(F32)
    mid = (whole - top).astype(BF16).astype(F32)
    low = whole - top - mid
    row = lax.broadcasted_iota(jnp.int32, (16, whole.shape[1]), 0)
    zero = jnp.zeros_like(row, F32)
    return jnp.where(
        row == 0, top, jnp.where(row == 1, mid, jnp.where(row == 2, low, zero))
    ).astype(BF16)


def decay_of(payload, state):
    rows = payload[state : state + 16].astype(F32)
    return rows[0:1] + rows[1:2] + rows[2:3]


def chip_kernel(at_ref, own_ref, other_ref, out_ref):
    core = at_ref[1]
    half = out_ref.shape[1]
    state = own_ref.shape[0] - 16
    cols = pl.ds(pl.multiple_of(core * half, half), half)
    own, other = own_ref[:, cols], other_ref[:, cols]
    own_decay, other_decay = decay_of(own, state), decay_of(other, state)
    own_s, other_s = own[:state].astype(F32), other[:state].astype(F32)
    late = jnp.where(core == 1, own_decay, other_decay)
    first = jnp.where(core == 1, other_s, own_s)
    second = jnp.where(core == 1, own_s, other_s)
    out_ref[0:state] = (late * first + second).astype(BF16)
    out_ref[state : state + 16] = decay_rows(own_decay * other_decay)


def prefix_kernel(one_ref, two_ref, three_ref, out_ref):
    state = out_ref.shape[0]
    one, two, three = one_ref[...], two_ref[...], three_ref[...]
    total = two[:state].astype(F32) + decay_of(two, state) * three[:state].astype(F32)
    total = one[:state].astype(F32) + decay_of(one, state) * total
    out_ref[...] = total.astype(BF16)


def diag_kernel(xs_ref, bc_ref, s0_ref, ec_ref, z_ref, y_ref, gate_ref):
    rows, width = xs_ref.shape
    state = bc_ref.shape[1] // 2
    seen = lax.broadcasted_iota(jnp.int32, (SPAN, SPAN), 0) >= lax.broadcasted_iota(
        jnp.int32, (SPAN, SPAN), 1
    )
    for s in range(0, rows, SPAN):
        b, c = bc_ref[s : s + SPAN, :state], bc_ref[s : s + SPAN, state:]
        scores = jnp.where(seen, dot(c, b, ((1,), (1,))), 0.0).astype(BF16)
        y = dot(scores, xs_ref[s : s + SPAN])
        if s:
            y = y + dot(c, s0_ref[...])
        y_ref[s : s + SPAN] = y
    z = z_ref[...].astype(F32)
    gate_ref[...] = z * jax.nn.sigmoid(z) * spread(ec_ref[...], width)


def gate_kernel(
    at_ref, mine_ref, theirs_ref, other_ref, bc_ref, y_ref, gate_ref, e0_ref, out_ref, ss_ref
):
    core = at_ref[1]
    state, half = mine_ref.shape
    mine, theirs = mine_ref[...].astype(F32), theirs_ref[...].astype(F32)
    left = jnp.where(core == 0, mine, theirs)
    right = jnp.where(core == 0, theirs, mine)
    prior = jnp.concatenate([left, right], 1)
    other = other_ref[...]
    after = decay_of(other, state) * prior + other[:state].astype(F32)
    incoming = jnp.where(core == 1, after, prior)
    ones = jnp.ones((8, out_ref.shape[1]), BF16)
    for n, s in enumerate(range(0, bc_ref.shape[0], SPAN)):
        start = incoming if n == 0 else incoming * e0_ref[0:1]
        y = y_ref[s : s + SPAN] + dot(bc_ref[s : s + SPAN, state:], start.astype(BF16))
        gated = y * gate_ref[s : s + SPAN]
        out_ref[s : s + SPAN] = gated
        top, mid, _ = thirds(gated * gated)
        ss_ref[:, s : s + SPAN] = dot(ones, top, ((1,), (1,))) + dot(ones, mid, ((1,), (1,)))


def part_order(px, core):
    return [2 * px + core, 2 * px + 1 - core, 2 * (1 - px) + core, 2 * (1 - px) + 1 - core]


def ahead_kernel(at_ref, *refs):
    out_ref = refs[-1]
    feats = out_ref.shape[3]
    for y, w_ref in enumerate(refs[:-1]):
        for j in range(out_ref.shape[1]):
            out_ref[y, j] = w_ref[:, j * feats : (j + 1) * feats]


def own_kernel(at_ref, w_ref, out_ref):
    feats = out_ref.shape[2]
    for j in range(out_ref.shape[0]):
        out_ref[j] = w_ref[:, j * feats : (j + 1) * feats]


def sort_kernel(at_ref, one_ref, two_ref, three_ref, all_ref, low_ref, high_ref):
    half = low_ref.shape[2]
    for d, ref in enumerate((one_ref, two_ref, three_ref)):
        piece = ref[0]
        all_ref[d] = piece
        low_ref[d] = piece[:, :half]
        high_ref[d] = piece[:, half:]


def norm_kernel(group_width, gated_ref, gain_ref, s0_ref, s1_ref, s2_ref, s3_ref, out_ref):
    mean_sq = (s0_ref[...] + s1_ref[...] + s2_ref[...] + s3_ref[...]) / group_width
    scale = spread(lax.rsqrt(mean_sq + norm_eps)[0:1], 128)
    for k in range(0, out_ref.shape[1], 128):
        piece = gated_ref[:, k : k + 128] * scale * gain_ref[:, k : k + 128]
        out_ref[:, k : k + 128] = piece.astype(BF16)


def project_kernel(at_ref, n0_ref, n1_ref, low_ref, high_ref, n3_ref, w0_ref, *refs):
    pieces, out_refs = refs[:6], refs[6:]
    part = n0_ref.shape[1] // 4
    rows, weights = [n0_ref[...]], [w0_ref[0]]
    for d, n_refs in enumerate(((n1_ref,), (low_ref, high_ref), (n3_ref,))):
        for p in part_order(at_ref[4], at_ref[1]):
            cols = pl.ds(pl.multiple_of(p * part, part), part)
            rows.append(jnp.concatenate([n[:, cols] for n in n_refs], 0))
        weights += [p[d, 0] for p in pieces]
    total = dot(jnp.concatenate(rows, 1), jnp.concatenate(weights, 0))
    if len(out_refs) == 1:
        out_refs[0][0] = total.astype(BF16)
    else:
        mid = out_refs[0].shape[0]
        out_refs[0][...] = total[:mid].astype(BF16)
        out_refs[1][...] = total[mid:].astype(BF16)


def call(body, at, ins, outs, scratch=(), specs=None, grid=(1,), out_specs=None, flops=0, vmem=48, pin=False):
    block = lambda v: pl.BlockSpec(v.shape, lambda *_, n=len(v.shape): (0,) * n)
    full = (lambda _: pl.BlockSpec(memory_space=pltpu.VMEM)) if pin else block
    specs = specs or {}
    in_specs = [specs.get(k) or full(a) for k, a in enumerate(ins)]
    kwargs = dict(
        out_shape=outs,
        compiler_params=pltpu.CompilerParams(vmem_limit_bytes=vmem << 20),
        cost_estimate=pl.CostEstimate(
            flops=flops,
            bytes_accessed=sum(a.size * a.dtype.itemsize for a in (*ins, *outs)),
            transcendentals=0,
        ),
    )
    if out_specs is None:
        out_specs = [block(o) for o in outs]
    if at is None:
        return pl.pallas_call(
            body, grid=grid, in_specs=in_specs, out_specs=out_specs, scratch_shapes=scratch, **kwargs
        )(*ins)
    return pl.pallas_call(
        body,
        grid_spec=pltpu.PrefetchScalarGridSpec(
            num_scalar_prefetch=1, grid=grid, in_specs=in_specs, out_specs=out_specs, scratch_shapes=scratch
        ),
        **kwargs,
    )(at, *ins)


def like(shape, dtype):
    return jax.ShapeDtypeStruct(shape, dtype)


def on_device(x, bc, z_gate, dt, rate, wx, wbc, gain, w_out):
    rows, width = x.shape
    heads = rate.shape[0]
    cols = bc.shape[1] // GROUPS
    state = cols // 2
    head_at, seq_at = lax.axis_index("head"), lax.axis_index("seq")
    group, core, y_at, z_at = head_at // QUAD, seq_at % CORES, head_at // NZ, head_at % NZ
    at = jnp.stack([group, core, y_at, z_at, seq_at // CORES % 2]).astype(jnp.int32)

    edge = lax.dynamic_slice(bc, (rows - RIM, group * cols), (RIM, cols))
    edges = jnp.concatenate([x[rows - RIM :], edge], 1)
    rim = lax.ppermute(edges, "seq", [(s, s + 1) for s in range(7)])

    quarter = w_out.shape[1] // NY
    feats = quarter // NZ
    part_k = width // 4
    at_late, _ = lax.optimization_barrier((at, edges))
    [ahead] = call(
        ahead_kernel,
        at_late,
        [w_out] * NY,
        [like((NY, NZ, part_k, feats), BF16)],
        specs={
            y: pl.BlockSpec((part_k, quarter), lambda i, s, y=y: (2 * s[4] + s[1], y))
            for y in range(NY)
        },
    )
    rim, ahead = lax.optimization_barrier((rim, ahead))
    columns = [[y * NZ + z for y in range(NY)] for z in range(NZ)]
    arrived = lax.all_to_all(ahead, "head", 0, 0, tiled=True, axis_index_groups=columns)

    block = pl.BlockSpec((rows, cols), lambda i, s: (0, s[0]))
    wblock = pl.BlockSpec((4, cols), lambda i, s: (0, s[0]))
    payload, xs, bc_conv, s0, grow, e0 = call(
        state_kernel,
        at,
        [x, bc, rim, wx, wbc, dt, rate[None, :]],
        [
            like((state + 16, width), BF16),
            like((rows, width), BF16),
            like((rows, cols), BF16),
            like((state, width), BF16),
            like((heads, rows), F32),
            like((8, width), F32),
        ],
        scratch=[pltpu.VMEM((rows + 8, width), F32), pltpu.VMEM((rows + 8, cols), F32)],
        specs={1: block, 4: wblock}
    )
    other = lax.ppermute(payload, "seq", CORE_SWAP)
    [chip] = call(chip_kernel, at, [payload, other], [like((state + 16, width // 2), BF16)])
    befores = [lax.ppermute(chip, "seq", x_route(d)) for d in (1, 2, 3)]
    y_local, gate = call(
        diag_kernel,
        None,
        [xs, bc_conv, s0, grow, z_gate],
        [like((rows, width), F32), like((rows, width), F32)],
    )
    before, y_local = lax.optimization_barrier((befores[0], y_local))
    befores[0] = before
    [mine] = call(prefix_kernel, None, befores, [like((state, width // 2), BF16)])
    theirs = lax.ppermute(mine, "seq", CORE_SWAP)

    gated, ss = call(
        gate_kernel,
        at,
        [mine, theirs, other, bc_conv, y_local, gate, e0],
        [like((rows, width), F32), like((8, rows), F32)],
    )
    more = [lax.ppermute(ss, "head", quad_route(d)) for d in range(1, QUAD)]
    at_then, _ = lax.optimization_barrier((at, ss))
    arrived_from = lambda d: pl.BlockSpec(
        (1, NZ, part_k, feats), lambda i, s: ((s[2] + NY - d) % NY, 0, 0, 0)
    )
    pair = (NY - 1, NZ, part_k // 2, feats)
    own, low, high = call(
        sort_kernel,
        at_then,
        [arrived] * (NY - 1),
        [like((NY - 1, NZ, part_k, feats), BF16), like(pair, BF16), like(pair, BF16)],
        specs={d - 1: arrived_from(d) for d in range(1, NY)},
    )
    ring = NX * CORES
    x_low = lax.ppermute(low, "seq", [(s, (s + CORES) % ring) for s in range(ring)])
    x_high = lax.ppermute(high, "seq", [(s, (s - CORES) % ring) for s in range(ring)])
    ss, _ = lax.optimization_barrier((ss, low))
    [normed] = call(
        functools.partial(norm_kernel, width * QUAD),
        None,
        [gated, gain[None, :], ss, *more],
        [like((rows, width), BF16)],
    )
    mid = rows // 2
    near_up, near_down = (lax.ppermute(normed, "head", y_route(d)) for d in (1, -1))
    far_low = lax.ppermute(near_up[:mid], "head", y_route(1))
    far_high = lax.ppermute(near_down[mid:], "head", y_route(-1))
    peers = [near_up, far_low, far_high, near_down]

    own_late, _ = lax.optimization_barrier((own, normed))
    at_own, _ = lax.optimization_barrier((at, normed))
    [w_own] = call(
        own_kernel,
        at_own,
        [w_out],
        [like((NZ, width, feats), BF16)],
        specs={0: pl.BlockSpec((width, quarter), lambda i, s: (0, s[2]))},
    )
    x_low, x_high, _, w_own = lax.optimization_barrier((x_low, x_high, near_up, w_own))
    swap = lambda v: lax.ppermute(v, "seq", CORE_SWAP)
    pieces = [own, swap(own_late), x_low, x_high, swap(x_low), swap(x_high)]

    def project(order, after):
        at_then, _ = lax.optimization_barrier((at, after))
        turn = lambda i: order[0] + sum(
            (b - a) * (i >= k + 1).astype(jnp.int32) for k, (a, b) in enumerate(zip(order, order[1:]))
        )
        piece = lambda v: pl.BlockSpec(
            (NY - 1, 1, v.shape[2], feats), lambda i, s: (0, (s[3] + turn(i)) % NZ, 0, 0)
        )
        own = pl.BlockSpec((1, width, feats), lambda i, s: ((s[3] + turn(i)) % NZ, 0, 0))
        if len(order) == 1:
            outs, out_specs = [like((rows // 2, feats), BF16)] * 2, None
        else:
            outs = [like((len(order), rows, feats), BF16)]
            out_specs = [pl.BlockSpec((1, rows, feats), lambda i, s: (i, 0, 0))]
        return call(
            project_kernel,
            at_then,
            [normed, *peers, w_own, *pieces],
            outs,
            specs={5: own, **{6 + k: piece(v) for k, v in enumerate(pieces)}},
            grid=(len(order),),
            out_specs=out_specs,
            flops=2 * rows * width * NY * feats * len(order),
            vmem=24,
            pin=True,
        )

    send = lambda v, d: lax.ppermute(v, "head", z_route(d))
    add = lambda a, b: (a.astype(F32) + b.astype(F32)).astype(BF16)
    far_up, far_down = project((4,), normed)
    up, down = send(far_up, 1), send(far_down, -1)
    [third] = project((3, 5), far_up)
    [second] = project((2, 6), (up, down))
    up = send(jnp.concatenate([add(third[0, :mid], up), third[0, mid:]], 0), 1)
    down = send(jnp.concatenate([third[1, :mid], add(third[1, mid:], down)], 0), -1)
    [first] = project((1, 7), (up, down))
    up, down = send(add(second[0], up), 1), send(add(second[1], down), -1)
    own_halves = project((0,), (up, down))
    up, down = send(add(first[0], up), 1), send(add(first[1], down), -1)
    own = jnp.concatenate(own_halves, 0)
    return (own.astype(F32) + up.astype(F32) + down.astype(F32)).astype(BF16).T


def solution(mesh):
    placed = (
        P("seq", "head"),
        P("seq", None),
        P("seq", "head"),
        P("head", "seq"),
        P("head"),
        P(None, "head"),
        P(),
        P("head"),
        P("head", None),
    )
    return jax.shard_map(
        on_device, mesh=mesh, in_specs=placed, out_specs=P("head", "seq"), check_vma=False
    )
```

```python
import functools

import jax
import jax.numpy as jnp
from jax import lax
from jax.experimental import pallas as pl
from jax.experimental.pallas import tpu as pltpu
from jax.sharding import PartitionSpec as P

GROUPS = 8
SPAN = 256
CORES = 2
NX = 4
NY = 4
NZ = 8
QUAD = 4
RIM = 16

norm_eps = 1e-05
F32 = jnp.float32
BF16 = jnp.bfloat16
EXACT = lax.Precision.HIGHEST


def y_route(dist):
    return [(y * NZ + z, (y + dist) % NY * NZ + z) for y in range(NY) for z in range(NZ)]


def z_route(dist):
    return [(y * NZ + z, y * NZ + (z + dist) % NZ) for y in range(NY) for z in range(NZ)]


def quad_route(dist):
    return [(h, h // QUAD * QUAD + (h + dist) % QUAD) for h in range(NY * NZ)]


def x_route(dist):
    return [(s, s + CORES * dist) for s in range(NX * CORES) if s + CORES * dist < NX * CORES]


CORE_SWAP = [(s, s ^ 1) for s in range(NX * CORES)]


def dot(a, b, dims=((1,), (0,)), precision=None):
    return lax.dot_general(a, b, (dims, ((), ())), precision=precision, preferred_element_type=F32)


def thirds(v):
    top = v.astype(BF16)
    rest = v - top.astype(F32)
    mid = rest.astype(BF16)
    return top, mid, (rest - mid.astype(F32)).astype(BF16)


def spread(heads_rows, width):
    heads = heads_rows.shape[0]
    pick = lax.broadcasted_iota(jnp.int32, (heads, width), 1) // (width // heads)
    own = lax.broadcasted_iota(jnp.int32, (heads, width), 0)
    pick = (pick == own).astype(F32)
    pick = jnp.concatenate([pick] * 3, 0).astype(BF16)
    parts = jnp.concatenate([p.astype(F32) for p in thirds(heads_rows)], 0).astype(BF16)
    return dot(parts, pick, ((0,), (0,)))


def conv(buf, src_ref, rim, w_ref):
    rows = src_ref.shape[0]
    buf[0:8] = rim
    buf[8 : rows + 8] = src_ref[...].astype(F32)
    taps = w_ref[...].astype(F32)
    run = taps[0:1] * buf[5 : 5 + rows]
    for k in range(1, 4):
        run = run + taps[k : k + 1] * buf[5 + k : 5 + k + rows]
    return (run * jax.nn.sigmoid(run)).astype(BF16)


def state_kernel(
    at_ref, x_ref, bc_ref, rim_ref, wx_ref, wbc_ref, dt_ref, rate_ref,
    pay_ref, xs_ref, bc_out, s0_ref, ec_ref, e0_ref, xbuf, bbuf,
):
    width = x_ref.shape[1]
    rows = x_ref.shape[0]
    state = bc_ref.shape[1] // 2
    rim = rim_ref[...].astype(F32)[RIM - 8 :]
    x_conv = conv(xbuf, x_ref, rim[:, :width], wx_ref)
    bc = conv(bbuf, bc_ref, rim[:, width:], wbc_ref)
    bc_out[...] = bc
    dt = dt_ref[...]
    own_row = lax.broadcasted_iota(jnp.int32, (dt.shape[0],) * 2, 0)
    own_row = own_row == lax.broadcasted_iota(jnp.int32, own_row.shape, 1)
    rate = jnp.sum(jnp.where(own_row, rate_ref[...], 0.0), 1, keepdims=True)
    steps = -rate * dt
    before = (
        lax.broadcasted_iota(jnp.int32, (SPAN, SPAN), 0)
        <= lax.broadcasted_iota(jnp.int32, (SPAN, SPAN), 1)
    ).astype(F32)
    cum = jnp.concatenate(
        [dot(steps[:, s : s + SPAN], before, precision=EXACT) for s in range(0, rows, SPAN)], 1
    )
    grow = jnp.exp(cum)
    ec_ref[...] = grow
    scale = spread(dt * jnp.exp(-cum), width)
    xs = (x_conv.astype(F32) * scale).astype(BF16)
    xs_ref[...] = xs
    b_all = bc[:, :state]
    lasts = jnp.concatenate([grow[:, SPAN - 1 : SPAN], grow[:, rows - 1 : rows]], 1)
    last = spread(lasts, width)
    s0 = last[0:1] * dot(b_all[:SPAN], xs[:SPAN], ((0,), (0,)))
    s1 = last[1:2] * dot(b_all[SPAN:], xs[SPAN:], ((0,), (0,)))
    s0_ref[...] = s0.astype(BF16)
    e0_ref[...] = jnp.broadcast_to(last[0:1], e0_ref.shape)
    pay_ref[0:state] = (last[1:2] * s0 + s1).astype(BF16)
    whole = last[0:1] * last[1:2]
    pay_ref[state : state + 16] = decay_rows(whole)


def decay_rows(whole):
    top = whole.astype(BF16).astype(F32)
    mid = (whole - top).astype(BF16).astype(F32)
    low = whole - top - mid
    row = lax.broadcasted_iota(jnp.int32, (16, whole.shape[1]), 0)
    zero = jnp.zeros_like(row, F32)
    return jnp.where(
        row == 0, top, jnp.where(row == 1, mid, jnp.where(row == 2, low, zero))
    ).astype(BF16)


def decay_of(payload, state):
    rows = payload[state : state + 16].astype(F32)
    return rows[0:1] + rows[1:2] + rows[2:3]


def chip_kernel(at_ref, own_ref, other_ref, out_ref):
    core = at_ref[1]
    half = out_ref.shape[1]
    state = own_ref.shape[0] - 16
    cols = pl.ds(pl.multiple_of(core * half, half), half)
    own, other = own_ref[:, cols], other_ref[:, cols]
    own_decay, other_decay = decay_of(own, state), decay_of(other, state)
    own_s, other_s = own[:state].astype(F32), other[:state].astype(F32)
    late = jnp.where(core == 1, own_decay, other_decay)
    first = jnp.where(core == 1, other_s, own_s)
    second = jnp.where(core == 1, own_s, other_s)
    out_ref[0:state] = (late * first + second).astype(BF16)
    out_ref[state : state + 16] = decay_rows(own_decay * other_decay)


def prefix_kernel(one_ref, two_ref, three_ref, out_ref):
    state = out_ref.shape[0]
    one, two, three = one_ref[...], two_ref[...], three_ref[...]
    total = two[:state].astype(F32) + decay_of(two, state) * three[:state].astype(F32)
    total = one[:state].astype(F32) + decay_of(one, state) * total
    out_ref[...] = total.astype(BF16)


def diag_kernel(xs_ref, bc_ref, s0_ref, ec_ref, z_ref, y_ref, gate_ref):
    rows, width = xs_ref.shape
    state = bc_ref.shape[1] // 2
    seen = lax.broadcasted_iota(jnp.int32, (SPAN, SPAN), 0) >= lax.broadcasted_iota(
        jnp.int32, (SPAN, SPAN), 1
    )
    for s in range(0, rows, SPAN):
        b, c = bc_ref[s : s + SPAN, :state], bc_ref[s : s + SPAN, state:]
        scores = jnp.where(seen, dot(c, b, ((1,), (1,))), 0.0).astype(BF16)
        y = dot(scores, xs_ref[s : s + SPAN])
        if s:
            y = y + dot(c, s0_ref[...])
        y_ref[s : s + SPAN] = y
    z = z_ref[...].astype(F32)
    gate_ref[...] = z * jax.nn.sigmoid(z) * spread(ec_ref[...], width)


def gate_kernel(
    at_ref, mine_ref, theirs_ref, other_ref, bc_ref, y_ref, gate_ref, e0_ref, out_ref, ss_ref
):
    core = at_ref[1]
    state, half = mine_ref.shape
    mine, theirs = mine_ref[...].astype(F32), theirs_ref[...].astype(F32)
    left = jnp.where(core == 0, mine, theirs)
    right = jnp.where(core == 0, theirs, mine)
    prior = jnp.concatenate([left, right], 1)
    other = other_ref[...]
    after = decay_of(other, state) * prior + other[:state].astype(F32)
    incoming = jnp.where(core == 1, after, prior)
    ones = jnp.ones((8, out_ref.shape[1]), BF16)
    for n, s in enumerate(range(0, bc_ref.shape[0], SPAN)):
        start = incoming if n == 0 else incoming * e0_ref[0:1]
        y = y_ref[s : s + SPAN] + dot(bc_ref[s : s + SPAN, state:], start.astype(BF16))
        gated = y * gate_ref[s : s + SPAN]
        out_ref[s : s + SPAN] = gated
        top, mid, _ = thirds(gated * gated)
        ss_ref[:, s : s + SPAN] = dot(ones, top, ((1,), (1,))) + dot(ones, mid, ((1,), (1,)))


def part_order(px, core):
    return [2 * px + core, 2 * px + 1 - core, 2 * (1 - px) + core, 2 * (1 - px) + 1 - core]


def ahead_kernel(at_ref, *refs):
    out_ref = refs[-1]
    feats = out_ref.shape[3]
    for y, w_ref in enumerate(refs[:-1]):
        for j in range(out_ref.shape[1]):
            out_ref[y, j] = w_ref[:, j * feats : (j + 1) * feats]


def own_kernel(at_ref, w_ref, out_ref):
    feats = out_ref.shape[2]
    for j in range(out_ref.shape[0]):
        out_ref[j] = w_ref[:, j * feats : (j + 1) * feats]


def sort_kernel(at_ref, one_ref, two_ref, three_ref, all_ref, low_ref, high_ref):
    half = low_ref.shape[2]
    for d, ref in enumerate((one_ref, two_ref, three_ref)):
        piece = ref[0]
        all_ref[d] = piece
        low_ref[d] = piece[:, :half]
        high_ref[d] = piece[:, half:]


def norm_kernel(group_width, gated_ref, gain_ref, s0_ref, s1_ref, s2_ref, s3_ref, out_ref):
    mean_sq = (s0_ref[...] + s1_ref[...] + s2_ref[...] + s3_ref[...]) / group_width
    scale = spread(lax.rsqrt(mean_sq + norm_eps)[0:1], 128)
    for k in range(0, out_ref.shape[1], 128):
        piece = gated_ref[:, k : k + 128] * scale * gain_ref[:, k : k + 128]
        out_ref[:, k : k + 128] = piece.astype(BF16)


def project_kernel(at_ref, n0_ref, n1_ref, low_ref, high_ref, n3_ref, w0_ref, *refs):
    pieces, out_refs = refs[:6], refs[6:]
    part = n0_ref.shape[1] // 4
    rows, weights = [n0_ref[...]], [w0_ref[0]]
    for d, n_refs in enumerate(((n1_ref,), (low_ref, high_ref), (n3_ref,))):
        for p in part_order(at_ref[4], at_ref[1]):
            cols = pl.ds(pl.multiple_of(p * part, part), part)
            rows.append(jnp.concatenate([n[:, cols] for n in n_refs], 0))
        weights += [p[d, 0] for p in pieces]
    total = dot(jnp.concatenate(rows, 1), jnp.concatenate(weights, 0))
    if len(out_refs) == 1:
        out_refs[0][0] = total.astype(BF16)
    else:
        mid = out_refs[0].shape[0]
        out_refs[0][...] = total[:mid].astype(BF16)
        out_refs[1][...] = total[mid:].astype(BF16)


def call(body, at, ins, outs, scratch=(), specs=None, grid=(1,), out_specs=None, flops=0, vmem=48, pin=False):
    block = lambda v: pl.BlockSpec(v.shape, lambda *_, n=len(v.shape): (0,) * n)
    full = (lambda _: pl.BlockSpec(memory_space=pltpu.VMEM)) if pin else block
    specs = specs or {}
    in_specs = [specs.get(k) or full(a) for k, a in enumerate(ins)]
    kwargs = dict(
        out_shape=outs,
        compiler_params=pltpu.CompilerParams(vmem_limit_bytes=vmem << 20),
        cost_estimate=pl.CostEstimate(
            flops=flops,
            bytes_accessed=sum(a.size * a.dtype.itemsize for a in (*ins, *outs)),
            transcendentals=0,
        ),
    )
    if out_specs is None:
        out_specs = [block(o) for o in outs]
    if at is None:
        return pl.pallas_call(
            body, grid=grid, in_specs=in_specs, out_specs=out_specs, scratch_shapes=scratch, **kwargs
        )(*ins)
    return pl.pallas_call(
        body,
        grid_spec=pltpu.PrefetchScalarGridSpec(
            num_scalar_prefetch=1, grid=grid, in_specs=in_specs, out_specs=out_specs, scratch_shapes=scratch
        ),
        **kwargs,
    )(at, *ins)


def like(shape, dtype):
    return jax.ShapeDtypeStruct(shape, dtype)


def on_device(x, bc, z_gate, dt, rate, wx, wbc, gain, w_out):
    rows, width = x.shape
    heads = rate.shape[0]
    cols = bc.shape[1] // GROUPS
    state = cols // 2
    head_at, seq_at = lax.axis_index("head"), lax.axis_index("seq")
    group, core, y_at, z_at = head_at // QUAD, seq_at % CORES, head_at // NZ, head_at % NZ
    at = jnp.stack([group, core, y_at, z_at, seq_at // CORES % 2]).astype(jnp.int32)

    edge = lax.dynamic_slice(bc, (rows - RIM, group * cols), (RIM, cols))
    edges = jnp.concatenate([x[rows - RIM :], edge], 1)
    rim = lax.ppermute(edges, "seq", [(s, s + 1) for s in range(7)])

    quarter = w_out.shape[1] // NY
    feats = quarter // NZ
    part_k = width // 4
    at_late, _ = lax.optimization_barrier((at, edges))
    [ahead] = call(
        ahead_kernel,
        at_late,
        [w_out] * NY,
        [like((NY, NZ, part_k, feats), BF16)],
        specs={
            y: pl.BlockSpec((part_k, quarter), lambda i, s, y=y: (2 * s[4] + s[1], y))
            for y in range(NY)
        },
    )
    rim, ahead = lax.optimization_barrier((rim, ahead))
    columns = [[y * NZ + z for y in range(NY)] for z in range(NZ)]
    arrived = lax.all_to_all(ahead, "head", 0, 0, tiled=True, axis_index_groups=columns)

    block = pl.BlockSpec((rows, cols), lambda i, s: (0, s[0]))
    wblock = pl.BlockSpec((4, cols), lambda i, s: (0, s[0]))
    payload, xs, bc_conv, s0, grow, e0 = call(
        state_kernel,
        at,
        [x, bc, rim, wx, wbc, dt, rate[None, :]],
        [
            like((state + 16, width), BF16),
            like((rows, width), BF16),
            like((rows, cols), BF16),
            like((state, width), BF16),
            like((heads, rows), F32),
            like((8, width), F32),
        ],
        scratch=[pltpu.VMEM((rows + 8, width), F32), pltpu.VMEM((rows + 8, cols), F32)],
        specs={1: block, 4: wblock}
    )
    other = lax.ppermute(payload, "seq", CORE_SWAP)
    [chip] = call(chip_kernel, at, [payload, other], [like((state + 16, width // 2), BF16)])
    befores = [lax.ppermute(chip, "seq", x_route(d)) for d in (1, 2, 3)]
    y_local, gate = call(
        diag_kernel,
        None,
        [xs, bc_conv, s0, grow, z_gate],
        [like((rows, width), F32), like((rows, width), F32)],
    )
    before, y_local = lax.optimization_barrier((befores[0], y_local))
    befores[0] = before
    [mine] = call(prefix_kernel, None, befores, [like((state, width // 2), BF16)])
    theirs = lax.ppermute(mine, "seq", CORE_SWAP)

    gated, ss = call(
        gate_kernel,
        at,
        [mine, theirs, other, bc_conv, y_local, gate, e0],
        [like((rows, width), F32), like((8, rows), F32)],
    )
    more = [lax.ppermute(ss, "head", quad_route(d)) for d in range(1, QUAD)]
    at_then, _ = lax.optimization_barrier((at, ss))
    arrived_from = lambda d: pl.BlockSpec(
        (1, NZ, part_k, feats), lambda i, s: ((s[2] + NY - d) % NY, 0, 0, 0)
    )
    pair = (NY - 1, NZ, part_k // 2, feats)
    own, low, high = call(
        sort_kernel,
        at_then,
        [arrived] * (NY - 1),
        [like((NY - 1, NZ, part_k, feats), BF16), like(pair, BF16), like(pair, BF16)],
        specs={d - 1: arrived_from(d) for d in range(1, NY)},
    )
    ring = NX * CORES
    x_low = lax.ppermute(low, "seq", [(s, (s + CORES) % ring) for s in range(ring)])
    x_high = lax.ppermute(high, "seq", [(s, (s - CORES) % ring) for s in range(ring)])
    ss, _ = lax.optimization_barrier((ss, low))
    [normed] = call(
        functools.partial(norm_kernel, width * QUAD),
        None,
        [gated, gain[None, :], ss, *more],
        [like((rows, width), BF16)],
    )
    mid = rows // 2
    near_up, near_down = (lax.ppermute(normed, "head", y_route(d)) for d in (1, -1))
    far_low = lax.ppermute(near_up[:mid], "head", y_route(1))
    far_high = lax.ppermute(near_down[mid:], "head", y_route(-1))
    peers = [near_up, far_low, far_high, near_down]

    own_late, _ = lax.optimization_barrier((own, normed))
    at_own, _ = lax.optimization_barrier((at, normed))
    [w_own] = call(
        own_kernel,
        at_own,
        [w_out],
        [like((NZ, width, feats), BF16)],
        specs={0: pl.BlockSpec((width, quarter), lambda i, s: (0, s[2]))},
    )
    x_low, x_high, _, w_own = lax.optimization_barrier((x_low, x_high, near_up, w_own))
    swap = lambda v: lax.ppermute(v, "seq", CORE_SWAP)
    pieces = [own, swap(own_late), x_low, x_high, swap(x_low), swap(x_high)]

    def project(order, after):
        at_then, _ = lax.optimization_barrier((at, after))
        turn = lambda i: order[0] + sum(
            (b - a) * (i >= k + 1).astype(jnp.int32) for k, (a, b) in enumerate(zip(order, order[1:]))
        )
        piece = lambda v: pl.BlockSpec(
            (NY - 1, 1, v.shape[2], feats), lambda i, s: (0, (s[3] + turn(i)) % NZ, 0, 0)
        )
        own = pl.BlockSpec((1, width, feats), lambda i, s: ((s[3] + turn(i)) % NZ, 0, 0))
        if len(order) == 1:
            outs, out_specs = [like((rows // 2, feats), BF16)] * 2, None
        else:
            outs = [like((len(order), rows, feats), BF16)]
            out_specs = [pl.BlockSpec((1, rows, feats), lambda i, s: (i, 0, 0))]
        return call(
            project_kernel,
            at_then,
            [normed, *peers, w_own, *pieces],
            outs,
            specs={5: own, **{6 + k: piece(v) for k, v in enumerate(pieces)}},
            grid=(len(order),),
            out_specs=out_specs,
            flops=2 * rows * width * NY * feats * len(order),
            vmem=24,
            pin=True,
        )

    send = lambda v, d: lax.ppermute(v, "head", z_route(d))
    add = lambda a, b: (a.astype(F32) + b.astype(F32)).astype(BF16)
    far_up, far_down = project((4,), normed)
    up, down = send(far_up, 1), send(far_down, -1)
    [third] = project((3, 5), far_up)
    [second] = project((2, 6), (up, down))
    after = lambda v, other: lax.optimization_barrier((v, other))[0]
    up_sum = jnp.concatenate([add(third[0, :mid], up), third[0, mid:]], 0)
    down_sum = jnp.concatenate([third[1, :mid], add(third[1, mid:], after(down, up_sum))], 0)
    up, down = send(up_sum, 1), send(down_sum, -1)
    [first] = project((1, 7), (up, down))
    up_sum = add(second[0], up)
    down_sum = add(second[1], after(down, up_sum))
    up, down = send(up_sum, 1), send(down_sum, -1)
    own_halves = project((0,), (up, down))
    up_sum = add(first[0], up)
    down_sum = add(first[1], after(down, up_sum))
    up, down = send(up_sum, 1), send(down_sum, -1)
    own = jnp.concatenate(own_halves, 0)
    return (own.astype(F32) + up.astype(F32) + down.astype(F32)).astype(BF16).T


def solution(mesh):
    placed = (
        P("seq", "head"),
        P("seq", None),
        P("seq", "head"),
        P("head", "seq"),
        P("head"),
        P(None, "head"),
        P(),
        P("head"),
        P("head", None),
    )
    return jax.shard_map(
        on_device, mesh=mesh, in_specs=placed, out_specs=P("head", "seq"), check_vma=False
    )
```
